32 devices in a mesh: parts: 2 (over y), seq: 4 (over z), tensor: 4 (over x, core).
Axes of the slice: x: 2, y: 2, z: 4, core: 2. Of those that a mesh axis runs over, the one named last changes fastest.
Arguments:
- query: bfloat16 [2048, 8192], P(('parts', 'seq'), 'tensor'), parts along dimension 0, may hold values from -6 to 6
- keys: bfloat16 [384, 1024], P(('parts', 'seq'), 'tensor'), parts along dimension 0, may hold values from -6 to 6
- values: bfloat16 [384, 1024], P(('parts', 'seq'), 'tensor'), parts along dimension 0, may hold values from -6 to 6
- q_gain: float32 [128], replicated, may hold values from 0.1 to 1.9
- key_norm_gain: float32 [128], replicated, may hold values from 0.1 to 1.9
- gate: float32 [64], P('tensor'), may hold values from 0.2 to 3
- grad_out: bfloat16 [2048, 8192], P(('parts', 'seq'), 'tensor'), parts along dimension 0, may hold values from -144 to 144
Outputs:
- query_grad: bfloat16 [2048, 8192], P(('parts', 'seq'), 'tensor'), parts along dimension 0
- projected_key_gradient: bfloat16 [384, 1024], P(('parts', 'seq'), 'tensor'), parts along dimension 0
- projected_value_gradient: bfloat16 [384, 1024], P(('parts', 'seq'), 'tensor'), parts along dimension 0
The draws below stay inside these ranges and needn't reach their ends.
There are 2 independent parts, one for each index of `parts`. The reference program is written for one: setup_inputs(seed, part) draws one part's arguments, and reference() takes and returns one part's arrays. A program takes and returns all parts, laid end to end along the dimension named above; an argument that names none is the same for every part. Nothing has to cross between parts.
All inputs are finite; a program needn't handle non-finite values.
Results may differ from the reference program's by a relative error of at most 0.0087.
Values may be sent and summed in bfloat16 or wider, within the bound.
A program may use at most 64 MiB of HBM per device.

```python
import math
import jax
import jax.numpy as jnp
from jax import lax

QUERY_HEADS = 64
KEY_VALUE_HEADS = 8
HEAD_SIZE = 128
TEXT = 1024
AUDIO_FRAMES = 192


def levels(own_key, dims, cuts, smallest, top_value):
    level, own = 1.0, jax.random.fold_in(own_key, 6)
    for position, blocks in cuts:
        draws = jnp.exp(jax.random.uniform(jax.random.fold_in(own, position), (blocks,), jnp.float32, smallest / len(cuts), top_value / len(cuts)))
        level = level * jnp.repeat(draws, dims[position] // blocks).reshape([-1 if axis == position else 1 for axis in range(len(dims))])
    return level


def centred(rng, dims, deviation, bound, split=(), kind=jnp.bfloat16):
    result = jax.random.normal(rng, dims, jnp.float32) * deviation
    if len(split) > 0:
        result = levels(rng, dims, split, -0.22, 0.18) * result
    return jnp.clip(result, min=-bound, max=bound).astype(kind)


def setup_inputs(seed: int = 0, part: int = 0) -> dict:
    key_list = jax.random.split(jax.random.key(seed), 8)
    part_splits = jax.random.split(jax.random.fold_in(key_list[7], part), 8)
    query = centred(part_splits[0], (TEXT, QUERY_HEADS * HEAD_SIZE), 1.0, 6.0, ((0, 4), (1, 4)))
    keys = centred(part_splits[1], (AUDIO_FRAMES, KEY_VALUE_HEADS * HEAD_SIZE), 1.0, 6.0, ((0, 4), (1, 4)))
    values = centred(part_splits[2], (AUDIO_FRAMES, KEY_VALUE_HEADS * HEAD_SIZE), 1.0, 6.0, ((0, 4), (1, 4)))
    q_gain = jnp.clip(1.0 + 0.18 * jax.random.normal(key_list[3], (HEAD_SIZE,), jnp.float32), 0.1, 1.9)
    key_norm_gain = jnp.clip(1.0 + 0.18 * jax.random.normal(key_list[4], (HEAD_SIZE,), jnp.float32), 0.1, 1.9)
    gate = jnp.clip(jnp.exp(math.log(3.0) - 2.7080502 * jax.random.uniform(key_list[5], (QUERY_HEADS,), jnp.float32) ** levels(key_list[5], (QUERY_HEADS,), ((0, 4),), -0.2, 0.2)), 0.2, 3.0)
    grad_out = centred(part_splits[6], (TEXT, QUERY_HEADS * HEAD_SIZE), 24.0, 144.0, ((0, 4), (1, 4)))
    return dict(query=query, keys=keys, values=values, q_gain=q_gain, key_norm_gain=key_norm_gain, gate=gate, grad_out=grad_out)


eps_value = 1e-05

def rms_norm_forward(raw, gain, head_count):
    count_rows = raw.shape[0]
    wide = raw.astype(jnp.float32).reshape(count_rows, head_count, raw.shape[1] // head_count)
    recip = lax.rsqrt(lax.optimization_barrier(jnp.mean(wide * wide, axis=-1, keepdims=True)) + eps_value)
    return (wide, recip, (wide * recip * gain).astype(jnp.bfloat16))

def rms_norm_backward(wide, recip, gain, upstream):
    scaled = gain * upstream
    return recip * scaled - wide * (recip * recip * recip) * lax.optimization_barrier(jnp.mean(wide * scaled, axis=-1, keepdims=True))

def reference(query, keys, values, q_gain, key_norm_gain, gate, grad_out):
    text_rows = query.shape[0]
    audio_frame_rows = keys.shape[0]
    head_group = QUERY_HEADS // KEY_VALUE_HEADS
    score_scale = 1.0 / math.sqrt(HEAD_SIZE)
    q_wide, q_recip, q_normed = rms_norm_forward(query, q_gain, QUERY_HEADS)
    key_widened, key_reciprocal, key_normalized = rms_norm_forward(keys, key_norm_gain, KEY_VALUE_HEADS)
    key_heads = key_normalized.transpose(1, 0, 2)
    heads_of_value = values.reshape(audio_frame_rows, KEY_VALUE_HEADS, HEAD_SIZE).transpose(1, 0, 2)
    go_wide = grad_out.astype(jnp.float32).reshape(text_rows, QUERY_HEADS, HEAD_SIZE) * jnp.tanh(gate)[None, :, None]
    go_half = go_wide.astype(jnp.bfloat16)

    def one_head(sliced):
        q_one, go_one, go_full, head_id = sliced
        kv_index = (head_id // head_group).astype(jnp.int32)
        k_one = lax.dynamic_index_in_dim(key_heads, kv_index, 0, keepdims=False)
        v_one = lax.dynamic_index_in_dim(heads_of_value, kv_index, 0, keepdims=False)
        logits = jnp.dot(q_one, k_one.T, preferred_element_type=jnp.float32) * score_scale
        exp_scores = jnp.exp(logits)
        row_sums = lax.optimization_barrier(jnp.sum(exp_scores, axis=1))
        output = jnp.dot(exp_scores.astype(jnp.bfloat16), v_one, preferred_element_type=jnp.float32) / row_sums[:, None]
        row_delta = lax.optimization_barrier(jnp.sum(go_full * output, axis=1))
        weights = exp_scores / row_sums[:, None]
        grad_probs = jnp.dot(go_one, v_one.T, preferred_element_type=jnp.float32)
        grad_scores = (weights * (grad_probs - row_delta[:, None])).astype(jnp.bfloat16)
        value_part = jnp.dot(weights.astype(jnp.bfloat16).T, go_one, preferred_element_type=jnp.float32)
        key_part = jnp.dot(grad_scores.T, q_one, preferred_element_type=jnp.float32) * score_scale
        query_part = jnp.dot(grad_scores, k_one, preferred_element_type=jnp.float32) * score_scale
        return (query_part, key_part, value_part)
    head_ids = jnp.arange(QUERY_HEADS, dtype=jnp.int32)
    query_parts, key_portions, value_portions = lax.map(one_head, (q_normed.transpose(1, 0, 2), go_half.transpose(1, 0, 2), go_wide.transpose(1, 0, 2), head_ids))
    key_gradient_sum = key_portions.reshape(KEY_VALUE_HEADS, head_group, audio_frame_rows, HEAD_SIZE).sum(axis=1).transpose(1, 0, 2)
    value_gradient_sum = value_portions.reshape(KEY_VALUE_HEADS, head_group, audio_frame_rows, HEAD_SIZE).sum(axis=1).transpose(1, 0, 2)
    query_grad = rms_norm_backward(q_wide, q_recip, q_gain, query_parts.transpose(1, 0, 2)).reshape(text_rows, QUERY_HEADS * HEAD_SIZE).astype(jnp.bfloat16)
    projected_key_gradient = rms_norm_backward(key_widened, key_reciprocal, key_norm_gain, key_gradient_sum).reshape(audio_frame_rows, KEY_VALUE_HEADS * HEAD_SIZE).astype(jnp.bfloat16)
    projected_value_gradient = value_gradient_sum.reshape(audio_frame_rows, KEY_VALUE_HEADS * HEAD_SIZE).astype(jnp.bfloat16)
    return (query_grad, projected_key_gradient, projected_value_gradient)
```

```python
import functools
import math

import jax
import jax.numpy as jnp
from jax import lax
from jax.experimental import pallas as pl
from jax.experimental.pallas import tpu as pltpu
from jax.sharding import PartitionSpec as P

HEAD_SIZE = 128
EPS = 1e-05
MESH = pl.DeviceIdType.MESH


def contract(a, b, dims):
    return lax.dot_general(a, b, (dims, ((), ())), preferred_element_type=jnp.float32)


def kernel(n, q_heads, kv_heads, text, rows,
           q_hbm, k_hbm, v_hbm, qg_ref, kg_ref, gate_ref, go_hbm,
           qout_ref, kout_ref, vout_ref,
           q_buf, go_buf, qn_buf, recip_buf, k_raw, kv_buf, gs_buf, acc, send_buf, recv_buf,
           q_sem, go_sem, kv_in_sem, g_send, g_recv, r_send, r_recv):
    me = lax.axis_index("seq")
    peers = [lax.rem(me + d, n) for d in range(1, n)]
    group = q_heads // kv_heads
    scale = 1.0 / math.sqrt(HEAD_SIZE)
    exp2_scale = scale * math.log2(math.e)
    mine = pl.ds(pl.multiple_of(me * rows, 16), rows)

    barrier = pltpu.get_barrier_semaphore()
    for p in peers:
        pl.semaphore_signal(barrier, inc=1, device_id={"seq": p}, device_id_type=MESH)

    def col(h):
        return pl.ds(pl.multiple_of(h * HEAD_SIZE, HEAD_SIZE), HEAD_SIZE)

    def q_copy(h):
        return pltpu.make_async_copy(q_hbm.at[:, col(h)], q_buf.at[h], q_sem.at[h])

    def go_copy(h):
        return pltpu.make_async_copy(go_hbm.at[:, col(h)], go_buf.at[h], go_sem.at[h])

    loads = []
    for c in range(kv_heads):
        loads.append(pltpu.make_async_copy(k_hbm.at[:, col(c)], k_raw.at[c], kv_in_sem.at[c]))
        loads.append(
            pltpu.make_async_copy(
                v_hbm.at[:, col(c)], kv_buf.at[kv_heads + c, mine, :], kv_in_sem.at[kv_heads + c]
            )
        )
    for copy in loads:
        copy.start()

    def start_inputs(h, carry):
        q_copy(h).start()
        go_copy(h).start()
        return carry

    lax.fori_loop(0, q_heads, start_inputs, 0)

    for copy in loads:
        copy.wait()
    for c in range(kv_heads):
        wide = k_raw[c].astype(jnp.float32)
        recip = lax.rsqrt(jnp.mean(wide * wide, axis=-1, keepdims=True) + EPS)
        kv_buf[c, mine, :] = (wide * recip * kg_ref[...]).astype(jnp.bfloat16)

    pl.semaphore_wait(barrier, n - 1)

    def gather_copy(d):
        return pltpu.make_async_remote_copy(
            src_ref=kv_buf.at[:, mine, :],
            dst_ref=kv_buf.at[:, mine, :],
            send_sem=g_send.at[d],
            recv_sem=g_recv.at[me],
            device_id={"seq": peers[d]},
            device_id_type=MESH,
        )

    def gather_landed(d):
        p = peers[d]
        there = pl.ds(pl.multiple_of(p * rows, 16), rows)
        return pltpu.make_async_remote_copy(
            src_ref=kv_buf.at[:, mine, :],
            dst_ref=kv_buf.at[:, there, :],
            send_sem=g_send.at[d],
            recv_sem=g_recv.at[p],
            device_id={"seq": p},
            device_id_type=MESH,
        )

    for d in range(n - 1):
        gather_copy(d).start()

    gates = jnp.tanh(gate_ref[...])
    lane = lax.broadcasted_iota(jnp.int32, gates.shape, 1)

    def prepare(h, carry):
        q_copy(h).wait()
        wide = q_buf[h].astype(jnp.float32)
        recip = lax.rsqrt(jnp.mean(wide * wide, axis=-1, keepdims=True) + EPS)
        recip_buf[h] = recip
        qn_buf[h] = (wide * recip * qg_ref[...]).astype(jnp.bfloat16)
        go_copy(h).wait()
        gate = jnp.sum(jnp.where(lane == h, gates, 0.0), axis=1, keepdims=True)
        go_buf[h] = (go_buf[h].astype(jnp.float32) * gate).astype(jnp.bfloat16)
        return carry

    lax.fori_loop(0, q_heads, prepare, 0)

    for d in range(n - 1):
        gather_landed(d).wait_recv()

    def reduce_copy(c, d):
        return pltpu.make_async_remote_copy(
            src_ref=send_buf.at[c, peers[d]],
            dst_ref=recv_buf.at[c, me],
            send_sem=r_send.at[c, d],
            recv_sem=r_recv.at[c, me],
            device_id={"seq": peers[d]},
            device_id_type=MESH,
        )

    def reduce_landed(c, d):
        return pltpu.make_async_remote_copy(
            src_ref=send_buf.at[c, peers[d]],
            dst_ref=recv_buf.at[c, peers[d]],
            send_sem=r_send.at[c, d],
            recv_sem=r_recv.at[c, peers[d]],
            device_id={"seq": peers[d]},
            device_id_type=MESH,
        )

    for c in range(kv_heads):
        acc[c] = jnp.zeros(acc.shape[1:], jnp.float32)

        def terms(i, carry):
            h = c * group + i
            qn = qn_buf[h]
            go = go_buf[h]
            logits = contract(kv_buf[c], qn, ((1,), (1,)))
            probs = contract(kv_buf[kv_heads + c], go, ((1,), (1,)))
            exps = jnp.exp2(logits * exp2_scale)
            inverse = 1.0 / jnp.sum(exps, axis=0, keepdims=True)
            weights = exps * inverse
            delta = jnp.sum(weights * probs, axis=0, keepdims=True)
            grads = (weights * (probs - delta)).astype(jnp.bfloat16)
            gs_buf[h] = grads
            acc[c, 1] += contract(weights.astype(jnp.bfloat16), go, ((1,), (0,)))
            acc[c, 0] += contract(grads, qn, ((1,), (0,)))
            return carry

        lax.fori_loop(0, group, terms, 0)
        for p in range(n):
            for t in range(2):
                send_buf[c, p, t] = acc[c, t, p * rows:(p + 1) * rows, :].astype(jnp.bfloat16)
        for d in range(n - 1):
            reduce_copy(c, d).start()

    for c in range(kv_heads):

        def query_side(i, carry):
            h = c * group + i
            upstream = contract(gs_buf[h], kv_buf[c], ((0,), (0,))) * scale
            wide = q_buf[h].astype(jnp.float32)
            recip = recip_buf[h]
            scaled = qg_ref[...] * upstream
            mean = jnp.mean(wide * scaled, axis=-1, keepdims=True)
            out = recip * scaled - wide * ((recip * recip * recip) * mean)
            qout_ref[:, col(h)] = out.astype(jnp.bfloat16)
            return carry

        lax.fori_loop(0, group, query_side, 0)

    for c in range(kv_heads):
        key_sum = acc[c, 0, mine, :]
        value_sum = acc[c, 1, mine, :]
        for d in range(n - 1):
            reduce_landed(c, d).wait_recv()
            key_sum += recv_buf[c, peers[d], 0].astype(jnp.float32)
            value_sum += recv_buf[c, peers[d], 1].astype(jnp.float32)
        wide = k_raw[c].astype(jnp.float32)
        recip = lax.rsqrt(jnp.mean(wide * wide, axis=-1, keepdims=True) + EPS)
        scaled = kg_ref[...] * (key_sum * scale)
        mean = jnp.mean(wide * scaled, axis=-1, keepdims=True)
        out = recip * scaled - wide * ((recip * recip * recip) * mean)
        lanes = slice(c * HEAD_SIZE, (c + 1) * HEAD_SIZE)
        kout_ref[:, lanes] = out.astype(jnp.bfloat16)
        vout_ref[:, lanes] = value_sum.astype(jnp.bfloat16)

    for d in range(n - 1):
        gather_copy(d).wait_send()
        for c in range(kv_heads):
            reduce_copy(c, d).wait_send()


def shards(n, query, keys, values, q_gain, key_norm_gain, gate, grad_out):
    text = query.shape[0]
    q_heads = query.shape[1] // HEAD_SIZE
    kv_heads = keys.shape[1] // HEAD_SIZE
    rows = keys.shape[0]
    frames = n * rows
    bf16, f32 = jnp.bfloat16, jnp.float32
    any_spec = pl.BlockSpec(memory_space=pl.ANY)
    vmem = pl.BlockSpec(memory_space=pltpu.VMEM)
    dma = pltpu.SemaphoreType.DMA
    return pl.pallas_call(
        functools.partial(kernel, n, q_heads, kv_heads, text, rows),
        out_shape=(
            jax.ShapeDtypeStruct(query.shape, bf16),
            jax.ShapeDtypeStruct(keys.shape, bf16),
            jax.ShapeDtypeStruct(values.shape, bf16),
        ),
        in_specs=[any_spec, any_spec, any_spec, vmem, vmem, vmem, any_spec],
        out_specs=(vmem, vmem, vmem),
        scratch_shapes=[
            pltpu.VMEM((q_heads, text, HEAD_SIZE), bf16),
            pltpu.VMEM((q_heads, text, HEAD_SIZE), bf16),
            pltpu.VMEM((q_heads, text, HEAD_SIZE), bf16),
            pltpu.VMEM((q_heads, text, 1), f32),
            pltpu.VMEM((kv_heads, rows, HEAD_SIZE), bf16),
            pltpu.VMEM((2 * kv_heads, frames, HEAD_SIZE), bf16),
            pltpu.VMEM((q_heads, frames, text), bf16),
            pltpu.VMEM((kv_heads, 2, frames, HEAD_SIZE), f32),
            pltpu.VMEM((kv_heads, n, 2, rows, HEAD_SIZE), bf16),
            pltpu.VMEM((kv_heads, n, 2, rows, HEAD_SIZE), bf16),
            dma((q_heads,)),
            dma((q_heads,)),
            dma((2 * kv_heads,)),
            dma((n,)),
            dma((n,)),
            dma((kv_heads, n)),
            dma((kv_heads, n)),
        ],
        compiler_params=pltpu.CompilerParams(
            collective_id=0, has_side_effects=True, vmem_limit_bytes=48 * 1024 * 1024
        ),
    )(query, keys, values, q_gain.reshape(1, -1), key_norm_gain.reshape(1, -1), gate.reshape(1, -1), grad_out)


def solution(mesh):
    wide = P(("parts", "seq"), "tensor")
    return jax.shard_map(
        functools.partial(shards, mesh.shape["seq"]),
        mesh=mesh,
        in_specs=(wide, wide, wide, P(), P(), P("tensor"), wide),
        out_specs=(wide, wide, wide),
        check_vma=False,
    )
```

```python
import functools
import math

import jax
import jax.numpy as jnp
from jax import lax
from jax.experimental import pallas as pl
from jax.experimental.pallas import tpu as pltpu
from jax.sharding import PartitionSpec as P

HEAD_SIZE = 128
EPS = 1e-05
MESH = pl.DeviceIdType.MESH
UNROLL = 4
VMEM_LIMIT = 62 * 1024 * 1024


def contract(a, b, dims):
    return lax.dot_general(a, b, (dims, ((), ())), preferred_element_type=jnp.float32)


def kernel(n, q_heads, kv_heads, text, rows,
           q_hbm, k_hbm, v_hbm, qg_hbm, kg_hbm, gate_hbm, go_hbm,
           qout_ref, kout_ref, vout_ref,
           qg_ref, kg_ref, gate_ref, q_buf, go_buf, qn_buf, recip_buf, k_raw, kv_buf, gs_buf, acc, send_buf, recv_buf,
           small_sem, q_sem, go_sem, kv_in_sem, g_send, g_recv, r_send, r_recv):
    me = lax.axis_index("seq")
    peers = [lax.rem(me + d, n) for d in range(1, n)]
    group = q_heads // kv_heads
    scale = 1.0 / math.sqrt(HEAD_SIZE)
    exp2_scale = scale * math.log2(math.e)
    mine = pl.ds(pl.multiple_of(me * rows, 16), rows)

    barrier = pltpu.get_barrier_semaphore()
    for p in peers:
        pl.semaphore_signal(barrier, inc=1, device_id={"seq": p}, device_id_type=MESH)

    def col(h):
        return pl.ds(pl.multiple_of(h * HEAD_SIZE, HEAD_SIZE), HEAD_SIZE)

    def q_copy(h):
        return pltpu.make_async_copy(q_hbm.at[:, col(h)], q_buf.at[h], q_sem.at[h])

    def go_copy(h):
        return pltpu.make_async_copy(go_hbm.at[:, col(h)], go_buf.at[h], go_sem.at[h])

    loads = [
        pltpu.make_async_copy(src, dst, small_sem.at[i])
        for i, (src, dst) in enumerate(
            ((kg_hbm, kg_ref), (qg_hbm, qg_ref), (gate_hbm, gate_ref))
        )
    ]
    for c in range(kv_heads):
        loads.append(pltpu.make_async_copy(k_hbm.at[:, col(c)], k_raw.at[c], kv_in_sem.at[c]))
        loads.append(
            pltpu.make_async_copy(
                v_hbm.at[:, col(c)], kv_buf.at[c, 1, mine, :], kv_in_sem.at[kv_heads + c]
            )
        )
    for copy in loads:
        copy.start()

    def start_inputs(h, carry):
        q_copy(h).start()
        go_copy(h).start()
        return carry

    lax.fori_loop(0, q_heads, start_inputs, 0)

    for copy in loads:
        copy.wait()
    for c in range(kv_heads):
        wide = k_raw[c].astype(jnp.float32)
        recip = lax.rsqrt(jnp.mean(wide * wide, axis=-1, keepdims=True) + EPS)
        kv_buf[c, 0, mine, :] = (wide * recip * kg_ref[...]).astype(jnp.bfloat16)

    pl.semaphore_wait(barrier, n - 1)

    def gather_copy(c, d):
        return pltpu.make_async_remote_copy(
            src_ref=kv_buf.at[c, :, mine, :],
            dst_ref=kv_buf.at[c, :, mine, :],
            send_sem=g_send.at[c, d],
            recv_sem=g_recv.at[c, me],
            device_id={"seq": peers[d]},
            device_id_type=MESH,
        )

    def gather_landed(c, d):
        p = peers[d]
        there = pl.ds(pl.multiple_of(p * rows, 16), rows)
        return pltpu.make_async_remote_copy(
            src_ref=kv_buf.at[c, :, mine, :],
            dst_ref=kv_buf.at[c, :, there, :],
            send_sem=g_send.at[c, d],
            recv_sem=g_recv.at[c, p],
            device_id={"seq": p},
            device_id_type=MESH,
        )

    for c in range(kv_heads):
        for d in range(n - 1):
            gather_copy(c, d).start()

    gates = jnp.tanh(gate_ref[...])
    lane = lax.broadcasted_iota(jnp.int32, gates.shape, 1)

    def prepare(step, carry):
        for u in range(UNROLL):
            h = step * UNROLL + u
            q_copy(h).wait()
            go_copy(h).wait()
        for u in range(UNROLL):
            h = step * UNROLL + u
            wide = q_buf[h].astype(jnp.float32)
            recip = lax.rsqrt(jnp.mean(wide * wide, axis=-1, keepdims=True) + EPS)
            recip_buf[h] = recip
            qn_buf[h] = (wide * recip * qg_ref[...]).astype(jnp.bfloat16)
            gate = jnp.sum(jnp.where(lane == h, gates, 0.0), axis=1, keepdims=True)
            go_buf[h] = (go_buf[h].astype(jnp.float32) * gate).astype(jnp.bfloat16)
        return carry

    lax.fori_loop(0, q_heads // UNROLL, prepare, 0)

    def reduce_copy(c, d):
        return pltpu.make_async_remote_copy(
            src_ref=send_buf.at[c, peers[d]],
            dst_ref=recv_buf.at[c, me],
            send_sem=r_send.at[c, d],
            recv_sem=r_recv.at[c, me],
            device_id={"seq": peers[d]},
            device_id_type=MESH,
        )

    def reduce_landed(c, d):
        return pltpu.make_async_remote_copy(
            src_ref=send_buf.at[c, peers[d]],
            dst_ref=recv_buf.at[c, peers[d]],
            send_sem=r_send.at[c, d],
            recv_sem=r_recv.at[c, peers[d]],
            device_id={"seq": peers[d]},
            device_id_type=MESH,
        )

    for c in range(kv_heads):
        acc[c] = jnp.zeros(acc.shape[1:], jnp.float32)
        for d in range(n - 1):
            gather_landed(c, d).wait_recv()

        def terms(step, carry):
            heads = [c * group + step * UNROLL + u for u in range(UNROLL)]
            qns = [qn_buf[h] for h in heads]
            gos = [go_buf[h] for h in heads]
            logits = [contract(kv_buf[c, 0], qn, ((1,), (1,))) for qn in qns]
            probs = [contract(kv_buf[c, 1], go, ((1,), (1,))) for go in gos]
            value_part, key_part = 0.0, 0.0
            for u, h in enumerate(heads):
                exps = jnp.exp2(logits[u] * exp2_scale)
                inverse = 1.0 / jnp.sum(exps, axis=0, keepdims=True)
                weights = exps * inverse
                delta = jnp.sum(weights * probs[u], axis=0, keepdims=True)
                grads = (weights * (probs[u] - delta)).astype(jnp.bfloat16)
                gs_buf[h] = grads
                value_part += contract(weights.astype(jnp.bfloat16), gos[u], ((1,), (0,)))
                key_part += contract(grads, qns[u], ((1,), (0,)))
            acc[c, 1] += value_part
            acc[c, 0] += key_part
            return carry

        lax.fori_loop(0, group // UNROLL, terms, 0)
        for p in range(n):
            for t in range(2):
                send_buf[c, p, t] = acc[c, t, p * rows:(p + 1) * rows, :].astype(jnp.bfloat16)
        for d in range(n - 1):
            reduce_copy(c, d).start()

    for c in range(kv_heads):

        def query_side(step, carry):
            for u in range(UNROLL):
                h = c * group + step * UNROLL + u
                upstream = contract(gs_buf[h], kv_buf[c, 0], ((0,), (0,))) * scale
                wide = q_buf[h].astype(jnp.float32)
                recip = recip_buf[h]
                scaled = qg_ref[...] * upstream
                mean = jnp.mean(wide * scaled, axis=-1, keepdims=True)
                out = recip * scaled - wide * ((recip * recip * recip) * mean)
                qout_ref[:, col(h)] = out.astype(jnp.bfloat16)
            return carry

        lax.fori_loop(0, group // UNROLL, query_side, 0)

    for c in range(kv_heads):
        key_sum = acc[c, 0, mine, :]
        value_sum = acc[c, 1, mine, :]
        for d in range(n - 1):
            reduce_landed(c, d).wait_recv()
            key_sum += recv_buf[c, peers[d], 0].astype(jnp.float32)
            value_sum += recv_buf[c, peers[d], 1].astype(jnp.float32)
        wide = k_raw[c].astype(jnp.float32)
        recip = lax.rsqrt(jnp.mean(wide * wide, axis=-1, keepdims=True) + EPS)
        scaled = kg_ref[...] * (key_sum * scale)
        mean = jnp.mean(wide * scaled, axis=-1, keepdims=True)
        out = recip * scaled - wide * ((recip * recip * recip) * mean)
        lanes = slice(c * HEAD_SIZE, (c + 1) * HEAD_SIZE)
        kout_ref[:, lanes] = out.astype(jnp.bfloat16)
        vout_ref[:, lanes] = value_sum.astype(jnp.bfloat16)

    for d in range(n - 1):
        for c in range(kv_heads):
            gather_copy(c, d).wait_send()
            reduce_copy(c, d).wait_send()


def shards(n, query, keys, values, q_gain, key_norm_gain, gate, grad_out):
    text = query.shape[0]
    q_heads = query.shape[1] // HEAD_SIZE
    kv_heads = keys.shape[1] // HEAD_SIZE
    rows = keys.shape[0]
    frames = n * rows
    bf16, f32 = jnp.bfloat16, jnp.float32
    any_spec = pl.BlockSpec(memory_space=pl.ANY)
    vmem = pl.BlockSpec(memory_space=pltpu.VMEM)
    dma = pltpu.SemaphoreType.DMA
    return pl.pallas_call(
        functools.partial(kernel, n, q_heads, kv_heads, text, rows),
        out_shape=(
            jax.ShapeDtypeStruct(query.shape, bf16),
            jax.ShapeDtypeStruct(keys.shape, bf16),
            jax.ShapeDtypeStruct(values.shape, bf16),
        ),
        in_specs=[any_spec] * 7,
        out_specs=(vmem, vmem, vmem),
        scratch_shapes=[
            pltpu.VMEM((1, HEAD_SIZE), f32),
            pltpu.VMEM((1, HEAD_SIZE), f32),
            pltpu.VMEM((1, q_heads), f32),
            pltpu.VMEM((q_heads, text, HEAD_SIZE), bf16),
            pltpu.VMEM((q_heads, text, HEAD_SIZE), bf16),
            pltpu.VMEM((q_heads, text, HEAD_SIZE), bf16),
            pltpu.VMEM((q_heads, text, 1), f32),
            pltpu.VMEM((kv_heads, rows, HEAD_SIZE), bf16),
            pltpu.VMEM((kv_heads, 2, frames, HEAD_SIZE), bf16),
            pltpu.VMEM((q_heads, frames, text), bf16),
            pltpu.VMEM((kv_heads, 2, frames, HEAD_SIZE), f32),
            pltpu.VMEM((kv_heads, n, 2, rows, HEAD_SIZE), bf16),
            pltpu.VMEM((kv_heads, n, 2, rows, HEAD_SIZE), bf16),
            dma((3,)),
            dma((q_heads,)),
            dma((q_heads,)),
            dma((2 * kv_heads,)),
            dma((kv_heads, n)),
            dma((kv_heads, n)),
            dma((kv_heads, n)),
            dma((kv_heads, n)),
        ],
        compiler_params=pltpu.CompilerParams(
            collective_id=0, has_side_effects=True, vmem_limit_bytes=VMEM_LIMIT
        ),
    )(query, keys, values, q_gain.reshape(1, -1), key_norm_gain.reshape(1, -1), gate.reshape(1, -1), grad_out)


def solution(mesh):
    wide = P(("parts", "seq"), "tensor")
    return jax.shard_map(
        functools.partial(shards, mesh.shape["seq"]),
        mesh=mesh,
        in_specs=(wide, wide, wide, P(), P(), P("tensor"), wide),
        out_specs=(wide, wide, wide),
        check_vma=False,
    )
```

```python
import functools
import math

import jax
import jax.numpy as jnp
from jax import lax
from jax.experimental import pallas as pl
from jax.experimental.pallas import tpu as pltpu
from jax.sharding import PartitionSpec as P

HEAD_SIZE = 128
EPS = 1e-05
MESH = pl.DeviceIdType.MESH
UNROLL = 4
VMEM_LIMIT = 62 * 1024 * 1024


def contract(a, b, dims):
    return lax.dot_general(a, b, (dims, ((), ())), preferred_element_type=jnp.float32)


def kernel(n, q_heads, kv_heads, text, rows,
           q_hbm, k_hbm, v_hbm, qg_hbm, kg_hbm, gate_hbm, go_hbm,
           qout_ref, kout_ref, vout_ref,
           qg_ref, kg_ref, gate_ref, q_buf, go_buf, qn_buf, recip_buf, k_raw, kv_buf, gs_buf, acc, send_buf, recv_buf,
           small_sem, q_sem, go_sem, kv_in_sem, g_send, g_recv, r_send, r_recv):
    me = lax.axis_index("seq")
    peers = [lax.rem(me + d, n) for d in range(1, n)]
    group = q_heads // kv_heads
    scale = 1.0 / math.sqrt(HEAD_SIZE)
    exp2_scale = scale * math.log2(math.e)
    mine = pl.ds(pl.multiple_of(me * rows, 16), rows)

    barrier = pltpu.get_barrier_semaphore()
    for p in peers:
        pl.semaphore_signal(barrier, inc=1, device_id={"seq": p}, device_id_type=MESH)

    def col(h):
        return pl.ds(pl.multiple_of(h * HEAD_SIZE, HEAD_SIZE), HEAD_SIZE)

    def q_copy(h):
        return pltpu.make_async_copy(q_hbm.at[:, col(h)], q_buf.at[h], q_sem.at[h])

    def go_copy(h):
        return pltpu.make_async_copy(go_hbm.at[:, col(h)], go_buf.at[h], go_sem.at[h])

    loads = [
        pltpu.make_async_copy(src, dst, small_sem.at[i])
        for i, (src, dst) in enumerate(
            ((kg_hbm, kg_ref), (qg_hbm, qg_ref), (gate_hbm, gate_ref))
        )
    ]
    for c in range(kv_heads):
        loads.append(pltpu.make_async_copy(k_hbm.at[:, col(c)], k_raw.at[c], kv_in_sem.at[c]))
        loads.append(
            pltpu.make_async_copy(
                v_hbm.at[:, col(c)], kv_buf.at[c, 1, mine, :], kv_in_sem.at[kv_heads + c]
            )
        )
    for copy in loads:
        copy.start()

    def start_inputs(h, carry):
        q_copy(h).start()
        go_copy(h).start()
        return carry

    lax.fori_loop(0, q_heads, start_inputs, 0)

    for copy in loads:
        copy.wait()
    for c in range(kv_heads):
        wide = k_raw[c].astype(jnp.float32)
        recip = lax.rsqrt(jnp.mean(wide * wide, axis=-1, keepdims=True) + EPS)
        kv_buf[c, 0, mine, :] = (wide * recip * kg_ref[...]).astype(jnp.bfloat16)

    pl.semaphore_wait(barrier, n - 1)

    def gather_copy(c, d):
        return pltpu.make_async_remote_copy(
            src_ref=kv_buf.at[c, :, mine, :],
            dst_ref=kv_buf.at[c, :, mine, :],
            send_sem=g_send.at[c, d],
            recv_sem=g_recv.at[c, me],
            device_id={"seq": peers[d]},
            device_id_type=MESH,
        )

    def gather_landed(c, d):
        p = peers[d]
        there = pl.ds(pl.multiple_of(p * rows, 16), rows)
        return pltpu.make_async_remote_copy(
            src_ref=kv_buf.at[c, :, mine, :],
            dst_ref=kv_buf.at[c, :, there, :],
            send_sem=g_send.at[c, d],
            recv_sem=g_recv.at[c, p],
            device_id={"seq": p},
            device_id_type=MESH,
        )

    for c in range(kv_heads):
        for d in range(n - 1):
            gather_copy(c, d).start()

    gates = jnp.tanh(gate_ref[...])
    lane = lax.broadcasted_iota(jnp.int32, gates.shape, 1)

    def prepare(step, carry):
        for u in range(UNROLL):
            h = step * UNROLL + u
            q_copy(h).wait()
            go_copy(h).wait()
        for u in range(UNROLL):
            h = step * UNROLL + u
            wide = q_buf[h].astype(jnp.float32)
            recip = lax.rsqrt(jnp.mean(wide * wide, axis=-1, keepdims=True) + EPS)
            recip_buf[h] = recip
            qn_buf[h] = (wide * recip * qg_ref[...]).astype(jnp.bfloat16)
            gate = jnp.sum(jnp.where(lane == h, gates, 0.0), axis=1, keepdims=True)
            go_buf[h] = (go_buf[h].astype(jnp.float32) * gate).astype(jnp.bfloat16)
        return carry

    lax.fori_loop(0, q_heads // UNROLL, prepare, 0)

    def reduce_copy(c, d):
        return pltpu.make_async_remote_copy(
            src_ref=send_buf.at[c, peers[d]],
            dst_ref=recv_buf.at[c, me],
            send_sem=r_send.at[c, d],
            recv_sem=r_recv.at[c, me],
            device_id={"seq": peers[d]},
            device_id_type=MESH,
        )

    def reduce_landed(c, d):
        return pltpu.make_async_remote_copy(
            src_ref=send_buf.at[c, peers[d]],
            dst_ref=recv_buf.at[c, peers[d]],
            send_sem=r_send.at[c, d],
            recv_sem=r_recv.at[c, peers[d]],
            device_id={"seq": peers[d]},
            device_id_type=MESH,
        )

    for c in range(kv_heads):
        acc[c] = jnp.zeros(acc.shape[1:], jnp.float32)
        for d in range(n - 1):
            gather_landed(c, d).wait_recv()

        def terms(step, carry):
            heads = [c * group + step * UNROLL + u for u in range(UNROLL)]
            qns = [qn_buf[h] for h in heads]
            gos = [go_buf[h] for h in heads]
            logits = [contract(kv_buf[c, 0], qn, ((1,), (1,))) for qn in qns]
            probs = [contract(kv_buf[c, 1], go, ((1,), (1,))) for go in gos]
            value_part, key_part = 0.0, 0.0
            for u, h in enumerate(heads):
                exps = jnp.exp2(logits[u] * exp2_scale)
                inverse = 1.0 / jnp.sum(exps, axis=0, keepdims=True)
                weights = exps * inverse
                delta = jnp.sum(weights * probs[u], axis=0, keepdims=True)
                grads = (weights * (probs[u] - delta)).astype(jnp.bfloat16)
                gs_buf[h] = grads
                value_part += contract(weights.astype(jnp.bfloat16), gos[u], ((1,), (0,)))
                key_part += contract(grads, qns[u], ((1,), (0,)))
            acc[c, 1] += value_part
            acc[c, 0] += key_part
            return carry

        lax.fori_loop(0, group // UNROLL, terms, 0)
        for p in range(n):
            for t in range(2):
                send_buf[c, p, t] = acc[c, t, p * rows:(p + 1) * rows, :].astype(jnp.bfloat16)
        for d in range(n - 1):
            reduce_copy(c, d).start()

    for c in range(kv_heads):

        def query_side(step, carry):
            for u in range(UNROLL):
                h = c * group + step * UNROLL + u
                upstream = contract(gs_buf[h], kv_buf[c, 0], ((0,), (0,))) * scale
                wide = q_buf[h].astype(jnp.float32)
                recip = recip_buf[h]
                scaled = qg_ref[...] * upstream
                mean = jnp.mean(wide * scaled, axis=-1, keepdims=True)
                out = recip * scaled - wide * ((recip * recip * recip) * mean)
                qout_ref[:, col(h)] = out.astype(jnp.bfloat16)
            return carry

        lax.fori_loop(0, group // UNROLL, query_side, 0)

    for c in range(kv_heads):
        key_sum = acc[c, 0, mine, :]
        value_sum = acc[c, 1, mine, :]
        for d in range(n - 1):
            reduce_landed(c, d).wait_recv()
            key_sum += recv_buf[c, peers[d], 0].astype(jnp.float32)
            value_sum += recv_buf[c, peers[d], 1].astype(jnp.float32)
        wide = k_raw[c].astype(jnp.float32)
        recip = lax.rsqrt(jnp.mean(wide * wide, axis=-1, keepdims=True) + EPS)
        scaled = kg_ref[...] * (key_sum * scale)
        mean = jnp.mean(wide * scaled, axis=-1, keepdims=True)
        out = recip * scaled - wide * ((recip * recip * recip) * mean)
        lanes = slice(c * HEAD_SIZE, (c + 1) * HEAD_SIZE)
        kout_ref[:, lanes] = out.astype(jnp.bfloat16)
        vout_ref[:, lanes] = value_sum.astype(jnp.bfloat16)

    for d in range(n - 1):
        for c in range(kv_heads):
            gather_copy(c, d).wait_send()
            reduce_copy(c, d).wait_send()


def write_out(q_in, k_in, v_in, q_out, k_out, v_out, sem):
    pairs = ((q_in, q_out), (k_in, k_out), (v_in, v_out))
    copies = [pltpu.make_async_copy(a, b, sem.at[i]) for i, (a, b) in enumerate(pairs)]
    for copy in copies:
        copy.start()
    for copy in copies:
        copy.wait()


def shards(n, query, keys, values, q_gain, key_norm_gain, gate, grad_out):
    text = query.shape[0]
    q_heads = query.shape[1] // HEAD_SIZE
    kv_heads = keys.shape[1] // HEAD_SIZE
    rows = keys.shape[0]
    frames = n * rows
    bf16, f32 = jnp.bfloat16, jnp.float32
    any_spec = pl.BlockSpec(memory_space=pl.ANY)
    vmem = pl.BlockSpec(memory_space=pltpu.VMEM)
    dma = pltpu.SemaphoreType.DMA
    grads = pl.pallas_call(
        functools.partial(kernel, n, q_heads, kv_heads, text, rows),
        out_shape=(
            pltpu.VMEM(query.shape, bf16),
            pltpu.VMEM(keys.shape, bf16),
            pltpu.VMEM(values.shape, bf16),
        ),
        in_specs=[any_spec] * 7,
        out_specs=(vmem, vmem, vmem),
        scratch_shapes=[
            pltpu.VMEM((1, HEAD_SIZE), f32),
            pltpu.VMEM((1, HEAD_SIZE), f32),
            pltpu.VMEM((1, q_heads), f32),
            pltpu.VMEM((q_heads, text, HEAD_SIZE), bf16),
            pltpu.VMEM((q_heads, text, HEAD_SIZE), bf16),
            pltpu.VMEM((q_heads, text, HEAD_SIZE), bf16),
            pltpu.VMEM((q_heads, text, 1), f32),
            pltpu.VMEM((kv_heads, rows, HEAD_SIZE), bf16),
            pltpu.VMEM((kv_heads, 2, frames, HEAD_SIZE), bf16),
            pltpu.VMEM((q_heads, frames, text), bf16),
            pltpu.VMEM((kv_heads, 2, frames, HEAD_SIZE), f32),
            pltpu.VMEM((kv_heads, n, 2, rows, HEAD_SIZE), bf16),
            pltpu.VMEM((kv_heads, n, 2, rows, HEAD_SIZE), bf16),
            dma((3,)),
            dma((q_heads,)),
            dma((q_heads,)),
            dma((2 * kv_heads,)),
            dma((kv_heads, n)),
            dma((kv_heads, n)),
            dma((kv_heads, n)),
            dma((kv_heads, n)),
        ],
        compiler_params=pltpu.CompilerParams(
            collective_id=0, has_side_effects=True, vmem_limit_bytes=VMEM_LIMIT
        ),
    )(query, keys, values, q_gain.reshape(1, -1), key_norm_gain.reshape(1, -1), gate.reshape(1, -1), grad_out)
    return pl.pallas_call(
        write_out,
        out_shape=tuple(jax.ShapeDtypeStruct(g.shape, g.dtype) for g in grads),
        in_specs=[vmem] * 3,
        out_specs=(any_spec,) * 3,
        scratch_shapes=[dma((3,))],
    )(*(pltpu.with_memory_space_constraint(g, pltpu.VMEM) for g in grads))


def solution(mesh):
    wide = P(("parts", "seq"), "tensor")
    return jax.shard_map(
        functools.partial(shards, mesh.shape["seq"]),
        mesh=mesh,
        in_specs=(wide, wide, wide, P(), P(), P("tensor"), wide),
        out_specs=(wide, wide, wide),
        check_vma=False,
    )
```

```python
import functools
import math

import jax
import jax.numpy as jnp
from jax import lax
from jax.experimental import pallas as pl
from jax.experimental.pallas import tpu as pltpu
from jax.sharding import PartitionSpec as P

HEAD_SIZE = 128
EPS = 1e-05
MESH = pl.DeviceIdType.MESH
UNROLL = 8
VMEM_LIMIT = 62 * 1024 * 1024


def contract(a, b, dims):
    return lax.dot_general(a, b, (dims, ((), ())), preferred_element_type=jnp.float32)


def kernel(n, q_heads, kv_heads, text, rows,
           q_hbm, k_hbm, v_hbm, qg_hbm, kg_hbm, gate_hbm, go_hbm,
           qout_ref, kout_ref, vout_ref,
           qg_ref, kg_ref, gate_ref, q_buf, go_buf, qn_buf, recip_buf, k_raw, kv_buf, gs_buf, acc, send_buf, recv_buf,
           small_sem, q_sem, go_sem, kv_in_sem, g_send, g_recv, r_send, r_recv):
    me = lax.axis_index("seq")
    peers = [lax.rem(me + d, n) for d in range(1, n)]
    group = q_heads // kv_heads
    scale = 1.0 / math.sqrt(HEAD_SIZE)
    exp2_scale = scale * math.log2(math.e)
    mine = pl.ds(pl.multiple_of(me * rows, 16), rows)

    barrier = pltpu.get_barrier_semaphore()
    for p in peers:
        pl.semaphore_signal(barrier, inc=1, device_id={"seq": p}, device_id_type=MESH)

    def col(h):
        return pl.ds(pl.multiple_of(h * HEAD_SIZE, HEAD_SIZE), HEAD_SIZE)

    def q_copy(h):
        return pltpu.make_async_copy(q_hbm.at[:, col(h)], q_buf.at[h], q_sem.at[h])

    def go_copy(h):
        return pltpu.make_async_copy(go_hbm.at[:, col(h)], go_buf.at[h], go_sem.at[h])

    loads = [
        pltpu.make_async_copy(src, dst, small_sem.at[i])
        for i, (src, dst) in enumerate(
            ((kg_hbm, kg_ref), (qg_hbm, qg_ref), (gate_hbm, gate_ref))
        )
    ]
    for c in range(kv_heads):
        loads.append(pltpu.make_async_copy(k_hbm.at[:, col(c)], k_raw.at[c], kv_in_sem.at[c]))
        loads.append(
            pltpu.make_async_copy(
                v_hbm.at[:, col(c)], kv_buf.at[c, 1, mine, :], kv_in_sem.at[kv_heads + c]
            )
        )
    for copy in loads:
        copy.start()

    def start_inputs(h, carry):
        q_copy(h).start()
        go_copy(h).start()
        return carry

    for copy in loads:
        copy.wait()
    for c in range(kv_heads):
        wide = k_raw[c].astype(jnp.float32)
        recip = lax.rsqrt(jnp.mean(wide * wide, axis=-1, keepdims=True) + EPS)
        kv_buf[c, 0, mine, :] = (wide * recip * kg_ref[...]).astype(jnp.bfloat16)

    pl.semaphore_wait(barrier, n - 1)

    def gather_copy(c, d):
        return pltpu.make_async_remote_copy(
            src_ref=kv_buf.at[c, :, mine, :],
            dst_ref=kv_buf.at[c, :, mine, :],
            send_sem=g_send.at[c, d],
            recv_sem=g_recv.at[c, me],
            device_id={"seq": peers[d]},
            device_id_type=MESH,
        )

    def gather_landed(c, d):
        p = peers[d]
        there = pl.ds(pl.multiple_of(p * rows, 16), rows)
        return pltpu.make_async_remote_copy(
            src_ref=kv_buf.at[c, :, mine, :],
            dst_ref=kv_buf.at[c, :, there, :],
            send_sem=g_send.at[c, d],
            recv_sem=g_recv.at[c, p],
            device_id={"seq": p},
            device_id_type=MESH,
        )

    for c in range(kv_heads):
        for d in range(n - 1):
            gather_copy(c, d).start()

    lax.fori_loop(0, q_heads, start_inputs, 0)

    gates = jnp.tanh(gate_ref[...])
    lane = lax.broadcasted_iota(jnp.int32, gates.shape, 1)

    def prepare(step, carry):
        for u in range(UNROLL):
            h = step * UNROLL + u
            q_copy(h).wait()
            go_copy(h).wait()
        for u in range(UNROLL):
            h = step * UNROLL + u
            wide = q_buf[h].astype(jnp.float32)
            recip = lax.rsqrt(jnp.mean(wide * wide, axis=-1, keepdims=True) + EPS)
            recip_buf[h] = recip
            qn_buf[h] = (wide * recip * qg_ref[...]).astype(jnp.bfloat16)
            gate = jnp.sum(jnp.where(lane == h, gates, 0.0), axis=1, keepdims=True)
            go_buf[h] = (go_buf[h].astype(jnp.float32) * gate).astype(jnp.bfloat16)
        return carry

    lax.fori_loop(0, q_heads // UNROLL, prepare, 0)

    def reduce_copy(c, d):
        return pltpu.make_async_remote_copy(
            src_ref=send_buf.at[c, peers[d]],
            dst_ref=recv_buf.at[c, me],
            send_sem=r_send.at[c, d],
            recv_sem=r_recv.at[c, me],
            device_id={"seq": peers[d]},
            device_id_type=MESH,
        )

    def reduce_landed(c, d):
        return pltpu.make_async_remote_copy(
            src_ref=send_buf.at[c, peers[d]],
            dst_ref=recv_buf.at[c, peers[d]],
            send_sem=r_send.at[c, d],
            recv_sem=r_recv.at[c, peers[d]],
            device_id={"seq": peers[d]},
            device_id_type=MESH,
        )

    for c in range(kv_heads):
        acc[c] = jnp.zeros(acc.shape[1:], jnp.float32)
        for d in range(n - 1):
            gather_landed(c, d).wait_recv()

        def terms(step, carry):
            heads = [c * group + step * UNROLL + u for u in range(UNROLL)]
            qns = [qn_buf[h] for h in heads]
            gos = [go_buf[h] for h in heads]
            logits = [contract(kv_buf[c, 0], qn, ((1,), (1,))) for qn in qns]
            probs = [contract(kv_buf[c, 1], go, ((1,), (1,))) for go in gos]
            value_part, key_part = 0.0, 0.0
            for u, h in enumerate(heads):
                exps = jnp.exp2(logits[u] * exp2_scale)
                inverse = 1.0 / jnp.sum(exps, axis=0, keepdims=True)
                weights = exps * inverse
                delta = jnp.sum(weights * probs[u], axis=0, keepdims=True)
                grads = (weights * (probs[u] - delta)).astype(jnp.bfloat16)
                gs_buf[h] = grads
                value_part += contract(weights.astype(jnp.bfloat16), gos[u], ((1,), (0,)))
                key_part += contract(grads, qns[u], ((1,), (0,)))
            acc[c, 1] += value_part
            acc[c, 0] += key_part
            return carry

        lax.fori_loop(0, group // UNROLL, terms, 0)
        for p in range(n):
            for t in range(2):
                send_buf[c, p, t] = acc[c, t, p * rows:(p + 1) * rows, :].astype(jnp.bfloat16)
        for d in range(n - 1):
            reduce_copy(c, d).start()

    for c in range(kv_heads):

        def query_side(step, carry):
            for u in range(UNROLL):
                h = c * group + step * UNROLL + u
                upstream = contract(gs_buf[h], kv_buf[c, 0], ((0,), (0,))) * scale
                wide = q_buf[h].astype(jnp.float32)
                recip = recip_buf[h]
                scaled = qg_ref[...] * upstream
                mean = jnp.mean(wide * scaled, axis=-1, keepdims=True)
                out = recip * scaled - wide * ((recip * recip * recip) * mean)
                qout_ref[:, col(h)] = out.astype(jnp.bfloat16)
            return carry

        lax.fori_loop(0, group // UNROLL, query_side, 0)

    for c in range(kv_heads):
        key_sum = acc[c, 0, mine, :]
        value_sum = acc[c, 1, mine, :]
        for d in range(n - 1):
            reduce_landed(c, d).wait_recv()
            key_sum += recv_buf[c, peers[d], 0].astype(jnp.float32)
            value_sum += recv_buf[c, peers[d], 1].astype(jnp.float32)
        wide = k_raw[c].astype(jnp.float32)
        recip = lax.rsqrt(jnp.mean(wide * wide, axis=-1, keepdims=True) + EPS)
        scaled = kg_ref[...] * (key_sum * scale)
        mean = jnp.mean(wide * scaled, axis=-1, keepdims=True)
        out = recip * scaled - wide * ((recip * recip * recip) * mean)
        lanes = slice(c * HEAD_SIZE, (c + 1) * HEAD_SIZE)
        kout_ref[:, lanes] = out.astype(jnp.bfloat16)
        vout_ref[:, lanes] = value_sum.astype(jnp.bfloat16)

    for d in range(n - 1):
        for c in range(kv_heads):
            gather_copy(c, d).wait_send()
            reduce_copy(c, d).wait_send()


def write_out(q_in, k_in, v_in, q_out, k_out, v_out, sem):
    pairs = ((q_in, q_out), (k_in, k_out), (v_in, v_out))
    copies = [pltpu.make_async_copy(a, b, sem.at[i]) for i, (a, b) in enumerate(pairs)]
    for copy in copies:
        copy.start()
    for copy in copies:
        copy.wait()


def shards(n, query, keys, values, q_gain, key_norm_gain, gate, grad_out):
    text = query.shape[0]
    q_heads = query.shape[1] // HEAD_SIZE
    kv_heads = keys.shape[1] // HEAD_SIZE
    rows = keys.shape[0]
    frames = n * rows
    bf16, f32 = jnp.bfloat16, jnp.float32
    any_spec = pl.BlockSpec(memory_space=pl.ANY)
    vmem = pl.BlockSpec(memory_space=pltpu.VMEM)
    dma = pltpu.SemaphoreType.DMA
    grads = pl.pallas_call(
        functools.partial(kernel, n, q_heads, kv_heads, text, rows),
        out_shape=(
            pltpu.VMEM(query.shape, bf16),
            pltpu.VMEM(keys.shape, bf16),
            pltpu.VMEM(values.shape, bf16),
        ),
        in_specs=[any_spec] * 7,
        out_specs=(vmem, vmem, vmem),
        scratch_shapes=[
            pltpu.VMEM((1, HEAD_SIZE), f32),
            pltpu.VMEM((1, HEAD_SIZE), f32),
            pltpu.VMEM((1, q_heads), f32),
            pltpu.VMEM((q_heads, text, HEAD_SIZE), bf16),
            pltpu.VMEM((q_heads, text, HEAD_SIZE), bf16),
            pltpu.VMEM((q_heads, text, HEAD_SIZE), bf16),
            pltpu.VMEM((q_heads, text, 1), f32),
            pltpu.VMEM((kv_heads, rows, HEAD_SIZE), bf16),
            pltpu.VMEM((kv_heads, 2, frames, HEAD_SIZE), bf16),
            pltpu.VMEM((q_heads, frames, text), bf16),
            pltpu.VMEM((kv_heads, 2, frames, HEAD_SIZE), f32),
            pltpu.VMEM((kv_heads, n, 2, rows, HEAD_SIZE), bf16),
            pltpu.VMEM((kv_heads, n, 2, rows, HEAD_SIZE), bf16),
            dma((3,)),
            dma((q_heads,)),
            dma((q_heads,)),
            dma((2 * kv_heads,)),
            dma((kv_heads, n)),
            dma((kv_heads, n)),
            dma((kv_heads, n)),
            dma((kv_heads, n)),
        ],
        compiler_params=pltpu.CompilerParams(
            collective_id=0, has_side_effects=True, vmem_limit_bytes=VMEM_LIMIT
        ),
    )(query, keys, values, q_gain.reshape(1, -1), key_norm_gain.reshape(1, -1), gate.reshape(1, -1), grad_out)
    return pl.pallas_call(
        write_out,
        out_shape=tuple(jax.ShapeDtypeStruct(g.shape, g.dtype) for g in grads),
        in_specs=[vmem] * 3,
        out_specs=(any_spec,) * 3,
        scratch_shapes=[dma((3,))],
    )(*(pltpu.with_memory_space_constraint(g, pltpu.VMEM) for g in grads))


def solution(mesh):
    wide = P(("parts", "seq"), "tensor")
    return jax.shard_map(
        functools.partial(shards, mesh.shape["seq"]),
        mesh=mesh,
        in_specs=(wide, wide, wide, P(), P(), P("tensor"), wide),
        out_specs=(wide, wide, wide),
        check_vma=False,
    )
```
